256 devices in a mesh: section: 8 (over y, core), seq: 32 (over x, z).
Axes of the slice: x: 4, y: 4, z: 8, core: 2. Of those that a mesh axis runs over, the one named last changes fastest.
Arguments:
- queries: bfloat16 [8, 8192, 2560], P('section', 'seq'), may hold values from -200 to 200
- keys: bfloat16 [8, 8192, 512], P('section', 'seq'), may hold values from -4 to 4
- values: bfloat16 [8, 8192, 512], P('section', 'seq'), may hold values from -6 to 6
- lengths: int32 [8, 64], P('section'), may hold values from 1 to 1024, 8192 in all within a row
Outputs:
- handed: bfloat16 [8, 8192, 2560], P('section', 'seq')
The draws below stay inside these ranges and needn't reach their ends.
Inputs may be any that keep to these rules, and one draw needn't show every extreme that they name: `lengths`: each row sums to 8192; its longest episode has exactly 1024 positions.
All inputs are finite; a program needn't handle non-finite values.
Results may differ from the reference program's by a relative error of at most 0.003.
Values may be sent and summed in bfloat16 or wider, within the bound.
No kernel may reach another device: no remote copies, remote signals or barrier semaphores. Data moves between devices by JAX's collectives and lax.ppermute only.
A program may use at most 128 MiB of HBM per device.

```python
import math
import jax
import jax.numpy as jnp
import numpy as np
from jax import lax

TOK_DEV = 256
HEADS = 20
KV_HEADS = 4
HDIM = 128
REACH = 4
MOST = 1024
TOKENS = 8192
EPISODES = 64
N_SECTION = 8
N_SEQ = 32


def drawn_parts(key):
    base = jnp.clip(jax.random.normal(jax.random.fold_in(key, 101), (N_SECTION, TOKENS, KV_HEADS * HDIM), jnp.float32), -4.0, 4.0)
    return base


def draw_keys(key, part):
    base = drawn_parts(key)
    return base.astype(jnp.bfloat16)


def draw_queries(key, part):
    key = jax.random.fold_in(key, 9)
    fresh = jnp.clip(jax.random.normal(key, (N_SECTION, TOKENS, HEADS * HDIM), jnp.float32), -4.0, 4.0)
    return fresh.astype(jnp.bfloat16)


def block_levels(rng, extent, split, smallest, largest):
    loudness, own = 1.0, jax.random.fold_in(rng, 6)
    for dim, blocks in split:
        heights = jnp.exp(jax.random.uniform(jax.random.fold_in(own, dim), (blocks,), jnp.float32, smallest / len(split), largest / len(split)))
        loudness = loudness * jnp.repeat(heights, extent[dim] // blocks).reshape([-1 if axis == dim else 1 for axis in range(len(extent))])
    return loudness


def split_up(amount, total, bound, slope):
    weights = [(1 << 20) // math.isqrt(grade ** slope) + 1 for grade in range(2, amount + 1)]
    surplus, counts = total - bound - (amount - 1), [1] * (amount - 1)
    while surplus > 0:
        movable = [i for i in range(amount - 1) if counts[i] < bound]
        whole, budget = sum([weights[i] for i in movable]), surplus
        for i in movable:
            addition = min(bound - counts[i], max(1, budget * weights[i] // whole), surplus)
            counts[i] = counts[i] + addition
            surplus = surplus - addition
    return np.array([bound] + counts)


def ragged_sizes(rng, count, total, reach, skew):
    if count == 2:
        one = jax.random.randint(rng, (), max(1, total - reach), min(reach, total - 1) + 1)
        return jnp.stack([one, total - one])
    sizes = jnp.asarray(split_up(count, total, reach, skew), jnp.int32)
    pairs = (count - 1) // 2
    source_of, receiver = sizes[1:1 + 2 * pairs:2], sizes[2:2 + 2 * pairs:2]
    margin = jnp.minimum(source_of - 1, reach - receiver)
    shifted = jax.random.randint(jax.random.fold_in(rng, 1), (pairs,), 0, 1 << 20) % (margin + 1)
    sizes = sizes.at[1:1 + 2 * pairs:2].set(source_of - shifted).at[2:2 + 2 * pairs:2].set(receiver + shifted)
    return sizes[jax.random.permutation(jax.random.fold_in(rng, 2), count)]


def bell_draw(rng, shape, width, bound, split=(), kind=jnp.bfloat16):
    factor_of = block_levels(rng, shape, split, -0.22, 0.18) if split else 1.0
    entries = jax.random.normal(rng, shape, jnp.float32) * width * factor_of
    return jnp.minimum(jnp.maximum(entries, -bound), bound).astype(kind)


def setup_inputs(seed: int = 0) -> dict:
    arg_keys = jax.random.split(jax.random.key(seed), 5)
    queries = draw_queries(jax.random.fold_in(arg_keys[4], 71), 0)
    keys = draw_keys(jax.random.fold_in(arg_keys[4], 71), 0)
    values = bell_draw(arg_keys[2], (N_SECTION, TOKENS, KV_HEADS * HDIM), 1.0, 6.0, ((0, 8), (1, 32)))
    lengths = jax.vmap(lambda own: ragged_sizes(own, EPISODES, TOKENS, MOST, 2))(jax.random.split(arg_keys[3], N_SECTION)).reshape((N_SECTION, EPISODES)).astype(jnp.int32)
    return {"queries": queries, "keys": keys, "values": values, "lengths": lengths}


LOWEST = -1.0e30


def first_starts(begins, positions):
    inside = begins[None, :] <= positions[:, None]
    return jnp.max(jnp.where(inside, begins[None, :], 0), axis=1).astype(jnp.int32)


def tile_terms(query_block, key_block, value_block, query_pos, key_pos, query_start, live):
    per_group = HEADS // KV_HEADS
    query_grid = query_block.astype(jnp.float32).reshape(TOK_DEV, KV_HEADS, per_group, HDIM)
    key_grid = key_block.astype(jnp.float32).reshape(TOK_DEV, KV_HEADS, HDIM)
    value_grid = value_block.astype(jnp.float32).reshape(TOK_DEV, KV_HEADS, HDIM)
    scores = jnp.einsum("qagd,kad->agqk", query_grid, key_grid) * (HDIM ** -0.5)
    visible = (key_pos[None, :] <= query_pos[:, None]) & (key_pos[None, :] >= query_start[:, None]) & live
    tile_max = jnp.max(jnp.where(visible, scores, LOWEST), axis=3)
    weights = jnp.where(visible, jnp.exp(scores - tile_max[..., None]), 0.0)
    tile_sum = jnp.sum(weights, axis=3)
    rounded = weights.astype(jnp.bfloat16).astype(jnp.float32)
    tile_out = jnp.einsum("agqk,kad->qagd", rounded, value_grid)
    return tile_out, tile_max, tile_sum


def merge_terms(terms):
    highest = terms[0][1]
    for item in terms[1:]:
        highest = jnp.maximum(highest, item[1])
    total_out = jnp.zeros_like(terms[0][0])
    total_sum = jnp.zeros_like(terms[0][2])
    for tile_out, tile_max, tile_sum in terms:
        factor = jnp.exp(tile_max - highest)
        total_out = total_out + tile_out * jnp.transpose(factor, (2, 0, 1))[..., None]
        total_sum = total_sum + tile_sum * factor
    return total_out, highest, total_sum


def section_attention(query_all, key_all, value_all, sizes_row):
    begins = (jnp.cumsum(sizes_row, dtype=jnp.int32) - sizes_row).astype(jnp.int32)
    positions = jnp.arange(TOKENS, dtype=jnp.int32)
    starts = first_starts(begins, positions)

    def one_block(block_index):
        offset = (block_index * TOK_DEV).astype(jnp.int32)
        query_block = lax.dynamic_slice_in_dim(query_all, offset, TOK_DEV, 0)
        query_pos = offset + jnp.arange(TOK_DEV, dtype=jnp.int32)
        query_start = lax.dynamic_slice_in_dim(starts, offset, TOK_DEV, 0)
        terms = []
        for back in range(REACH + 1):
            source = jnp.maximum(block_index - back, 0).astype(jnp.int32)
            key_offset = (source * TOK_DEV).astype(jnp.int32)
            key_block = lax.dynamic_slice_in_dim(key_all, key_offset, TOK_DEV, 0)
            value_block = lax.dynamic_slice_in_dim(value_all, key_offset, TOK_DEV, 0)
            key_pos = key_offset + jnp.arange(TOK_DEV, dtype=jnp.int32)
            terms.append(tile_terms(query_block, key_block, value_block, query_pos, key_pos, query_start, block_index - back >= 0))
        total_out, highest, total_sum = merge_terms(terms)
        finished = total_out / jnp.transpose(total_sum, (2, 0, 1))[..., None]
        return finished.astype(jnp.bfloat16).reshape(TOK_DEV, HEADS * HDIM)

    blocks = lax.map(one_block, jnp.arange(N_SEQ, dtype=jnp.int32))
    return blocks.reshape(TOKENS, HEADS * HDIM)


def reference(queries, keys, values, lengths):
    outputs = [section_attention(queries[section_index], keys[section_index], values[section_index], lengths[section_index]) for section_index in range(N_SECTION)]
    return jnp.roll(jnp.stack(outputs), 1, axis=0)
```

```python
from functools import partial

import jax
import jax.numpy as jnp
from jax import lax
from jax.experimental import pallas as pl
from jax.experimental.pallas import tpu as pltpu
from jax.sharding import PartitionSpec as P

HDIM = 128
KV_HEADS = 4
GROUP = 5
REACH = 4
LOWEST = -1e30
SCALE = HDIM**-0.5 * 1.4426950408889634


def moved(value, route):
    sections, blocks = lax.axis_size("section"), lax.axis_size("seq")
    pairs = []
    for s in range(sections):
        for b in range(blocks):
            s2, b2 = route(s, b)
            pairs.append((s * blocks + b, (s2 % sections) * blocks + b2 % blocks))
    return lax.ppermute(value, ("section", "seq"), pairs)


def step(blocks, sections=0):
    return lambda s, b: (s + sections, b + blocks)


def back_two(s, b):
    x, z = divmod(b, 8)
    return s + 1, x * 8 + (z - 2) % 8


def back_four(s, b):
    x, u = divmod(b, 8)
    return s, x * 8 + (u + 2) % 8 + 4


def tile(q, k, v, bias):
    raw = lax.dot_general(q, k, (((1,), (1,)), ((), ())), preferred_element_type=jnp.float32)
    raw = raw + bias
    top = jnp.max(raw, axis=1, keepdims=True)
    weights = jnp.exp2((raw - top) * SCALE)
    total = jnp.sum(weights, axis=1, keepdims=True)
    out = jnp.dot(weights.astype(jnp.bfloat16), v, preferred_element_type=jnp.float32)
    return out, top, total


def merged(terms):
    highest = terms[0][1]
    for item in terms[1:]:
        highest = jnp.maximum(highest, item[1])
    out, total = None, None
    for tile_out, top, tile_sum in terms:
        factor = jnp.exp2((top - highest) * SCALE)
        part, part_sum = tile_out * factor, tile_sum * factor
        out = part if out is None else out + part
        total = part_sum if total is None else total + part_sum
    return out, highest, total


def bias_of(starts, first_key, height):
    keys = first_key + lax.broadcasted_iota(jnp.int32, (height, height), 1)
    return jnp.where(keys >= starts, 0.0, LOWEST)


def near_kernel(index_ref, starts_ref, q_ref, *refs):
    count = 3
    ks, vs = refs[:count], refs[count : 2 * count]
    acc_ref, stat_ref, bias_ref = refs[2 * count :]
    height = q_ref.shape[0]

    @pl.when(pl.program_id(0) == 0)
    def _():
        starts = starts_ref[:, :1]
        first = index_ref[0] * height
        rows = lax.broadcasted_iota(jnp.int32, (height, height), 0)
        columns = lax.broadcasted_iota(jnp.int32, (height, height), 1)
        bias_ref[0] = jnp.where(columns <= rows, bias_of(starts, first, height), LOWEST)
        for back in range(1, count):
            bias_ref[back] = bias_of(starts, first - back * height, height)

    for g in range(GROUP):
        q = q_ref[:, g * HDIM : (g + 1) * HDIM]
        terms = [tile(q, ks[i][...], vs[i][...], bias_ref[i]) for i in range(count)]
        out, top, total = merged(terms)
        acc_ref[:, g * HDIM : (g + 1) * HDIM] = out
        stat_ref[:, g : g + 1] = top
        stat_ref[:, 8 + g : 9 + g] = total


def far_kernel(index_ref, starts_ref, q_ref, *refs):
    count = 2
    ks, vs = refs[:count], refs[count : 2 * count]
    acc_ref, stat_ref, out_ref, bias_ref = refs[2 * count :]
    height = q_ref.shape[0]

    @pl.when(pl.program_id(0) == 0)
    def _():
        starts = starts_ref[:, :1]
        first = index_ref[0] * height
        for back in range(3, 3 + count):
            bias_ref[back - 3] = bias_of(starts, first - back * height, height)

    for g in range(GROUP):
        q = q_ref[:, g * HDIM : (g + 1) * HDIM]
        terms = [(acc_ref[:, g * HDIM : (g + 1) * HDIM], stat_ref[:, g : g + 1], stat_ref[:, 8 + g : 9 + g])]
        terms += [tile(q, ks[i][...], vs[i][...], bias_ref[i]) for i in range(count)]
        out, _, total = merged(terms)
        out_ref[:, g * HDIM : (g + 1) * HDIM] = (out * (1.0 / total)).astype(out_ref.dtype)


def specs(height, count):
    wide = pl.BlockSpec((height, GROUP * HDIM), lambda a: (0, a))
    narrow = pl.BlockSpec((height, HDIM), lambda a: (0, a))
    whole = pl.BlockSpec((height, HDIM), lambda a: (0, 0))
    return wide, narrow, [pl.BlockSpec(memory_space=pltpu.SMEM), whole, wide] + [narrow] * (2 * count)


def cost(height, count):
    pairs = KV_HEADS * GROUP * height * height * count
    return pl.CostEstimate(flops=4 * HDIM * pairs, transcendentals=pairs, bytes_accessed=8 << 20)


def near(index, starts, q, ks, vs):
    height = q.shape[0]
    wide, narrow, inputs = specs(height, 3)
    return pl.pallas_call(
        near_kernel,
        grid=(KV_HEADS,),
        in_specs=inputs,
        out_specs=[wide, narrow],
        out_shape=[
            jax.ShapeDtypeStruct(q.shape, jnp.float32),
            jax.ShapeDtypeStruct((height, KV_HEADS * HDIM), jnp.float32),
        ],
        scratch_shapes=[pltpu.VMEM((3, height, height), jnp.float32)],
        compiler_params=pltpu.CompilerParams(vmem_limit_bytes=40 << 20),
        cost_estimate=cost(height, 3),
        name="near_tiles",
    )(index, starts, q, *ks, *vs)


def far(index, starts, q, ks, vs, acc, stat):
    height = q.shape[0]
    wide, narrow, inputs = specs(height, 2)
    return pl.pallas_call(
        far_kernel,
        grid=(KV_HEADS,),
        in_specs=inputs + [wide, narrow],
        out_specs=wide,
        out_shape=jax.ShapeDtypeStruct(q.shape, jnp.bfloat16),
        scratch_shapes=[pltpu.VMEM((2, height, height), jnp.float32)],
        compiler_params=pltpu.CompilerParams(vmem_limit_bytes=40 << 20),
        cost_estimate=cost(height, 2),
        name="far_tiles",
    )(index, starts, q, *ks, *vs, acc, stat)


def first_starts(sizes, positions):
    order = jnp.arange(sizes.shape[0], dtype=jnp.int32)
    begins = jnp.sum(jnp.where(order[:, None] < order[None, :], sizes[:, None], 0), axis=0, dtype=jnp.int32)
    inside = begins[None, :] <= positions[:, None]
    return jnp.max(jnp.where(inside, begins[None, :], 0), axis=1)


def body(queries, keys, values, lengths):
    q, k, v = queries[0], keys[0], values[0]
    height = q.shape[0]
    index = lax.axis_index("seq").astype(jnp.int32)

    v_far = moved(v, back_two)
    k1 = moved(k, step(1, 1))
    v1 = moved(v, step(1, 1))
    q0 = moved(q, step(0, 1))
    k0 = moved(k, step(0, 1))
    v0 = moved(v, step(0, 1))
    sizes = moved(lengths, step(0, 1))[0]
    k2 = moved(k1, step(1))
    v2 = moved(v1, step(1))
    v4 = moved(v_far, back_four)
    k3 = moved(k2, step(1))
    v3 = moved(v4, step(-1))
    k4 = moved(k3, step(1))

    positions = index * height + jnp.arange(height, dtype=jnp.int32)
    starts = jnp.broadcast_to(first_starts(sizes, positions)[:, None], (height, HDIM))
    index = index.reshape(1)
    acc, stat = near(index, starts, q0, [k0, k1, k2], [v0, v1, v2])
    return far(index, starts, q0, [k3, k4], [v3, v4], acc, stat)[None]


def solution(mesh):
    return jax.shard_map(
        body,
        mesh=mesh,
        in_specs=(
            P("section", "seq", None),
            P("section", "seq", None),
            P("section", "seq", None),
            P("section", None),
        ),
        out_specs=P("section", "seq", None),
        check_vma=False,
    )
```

```python
from functools import partial

import jax
import jax.numpy as jnp
from jax import lax
from jax.experimental import pallas as pl
from jax.experimental.pallas import tpu as pltpu
from jax.sharding import PartitionSpec as P

HDIM = 128
KV_HEADS = 4
GROUP = 5
REACH = 4
LOWEST = -1e30
SCALE = HDIM**-0.5 * 1.4426950408889634


def moved(value, route):
    sections, blocks = lax.axis_size("section"), lax.axis_size("seq")
    pairs = []
    for s in range(sections):
        for b in range(blocks):
            s2, b2 = route(s, b)
            pairs.append((s * blocks + b, (s2 % sections) * blocks + b2 % blocks))
    return lax.ppermute(value, ("section", "seq"), pairs)


def step(blocks, sections=0):
    return lambda s, b: (s + sections, b + blocks)


def back_two(s, b):
    x, z = divmod(b, 8)
    return s + 1, x * 8 + (z - 2) % 8


def back_four(s, b):
    x, u = divmod(b, 8)
    return s, x * 8 + (u + 2) % 8 + 4


def bias_of(starts, first_key, height):
    keys = first_key + lax.broadcasted_iota(jnp.int32, (height, height), 1)
    return jnp.where(keys >= starts, 0.0, LOWEST)


def tile(q, k, v, bias):
    height = bias.shape[0]
    raw = lax.dot_general(q, k, (((1,), (1,)), ((), ())), preferred_element_type=jnp.float32)
    raw = (raw.reshape(GROUP, height, height) + bias[None]).reshape(GROUP * height, height)
    top = jnp.max(raw, axis=1, keepdims=True)
    weights = jnp.exp2((raw - top) * SCALE)
    total = jnp.sum(weights, axis=1, keepdims=True)
    out = jnp.dot(weights.astype(jnp.bfloat16), v, preferred_element_type=jnp.float32)
    wide = (GROUP * height, HDIM)
    return out, jnp.broadcast_to(top, wide), jnp.broadcast_to(total, wide)


def merged(terms):
    highest = terms[0][1]
    for item in terms[1:]:
        highest = jnp.maximum(highest, item[1])
    out, total = None, None
    for tile_out, top, tile_sum in terms:
        factor = jnp.exp2((top - highest) * SCALE)
        part, part_sum = tile_out * factor, tile_sum * factor
        out = part if out is None else out + part
        total = part_sum if total is None else total + part_sum
    return out, highest, total


def kernel(backs, opening, closing, index_ref, starts_ref, q_ref, *refs):
    count = len(backs)
    ks, vs, refs = refs[:count], refs[count : 2 * count], refs[2 * count :]
    state_in = () if opening else refs[:3]
    outs, bias_ref = refs[len(state_in) : -1], refs[-1]
    height = q_ref.shape[0]
    starts = starts_ref[:, :1]
    first = index_ref[0] * height
    for i, back in enumerate(backs):
        bias = bias_of(starts, first - back * height, height)
        if back == 0:
            rows = lax.broadcasted_iota(jnp.int32, (height, height), 0)
            columns = lax.broadcasted_iota(jnp.int32, (height, height), 1)
            bias = jnp.where(columns <= rows, bias, LOWEST)
        bias_ref[i] = bias

    @pl.loop(0, KV_HEADS)
    def _(a):
        lanes = pl.ds(pl.multiple_of(a * HDIM, HDIM), HDIM)
        heads = [
            pl.ds(pl.multiple_of((a * GROUP + g) * HDIM, HDIM), HDIM) for g in range(GROUP)
        ]
        q = jnp.concatenate([q_ref[:, h] for h in heads], axis=0)
        terms = [tuple(ref[a] for ref in state_in)] if state_in else []
        terms += [tile(q, ks[i][:, lanes], vs[i][:, lanes], bias_ref[i]) for i in range(count)]
        result = merged(terms)
        if closing:
            done = (result[0] / result[2]).astype(jnp.bfloat16)
            for g in range(GROUP):
                outs[0][:, heads[g]] = done[g * height : (g + 1) * height]
        else:
            for ref, part in zip(outs, result):
                ref[a] = part


def attention(backs, index, starts, q, ks, vs, state=(), closing=False):
    height = q.shape[0]
    count = len(backs)
    pairs = KV_HEADS * GROUP * height * height * count
    vmem = pl.BlockSpec(memory_space=pltpu.VMEM)
    part = jax.ShapeDtypeStruct((KV_HEADS, GROUP * height, HDIM), jnp.float32)
    return pl.pallas_call(
        partial(kernel, backs, not state, closing),
        in_specs=[pl.BlockSpec(memory_space=pltpu.SMEM)] + [vmem] * (2 + 2 * count + len(state)),
        out_specs=vmem if closing else [vmem] * 3,
        out_shape=jax.ShapeDtypeStruct(q.shape, jnp.bfloat16) if closing else [part] * 3,
        scratch_shapes=[pltpu.VMEM((count, height, height), jnp.float32)],
        compiler_params=pltpu.CompilerParams(vmem_limit_bytes=12 << 20),
        cost_estimate=pl.CostEstimate(
            flops=4 * HDIM * pairs, transcendentals=pairs, bytes_accessed=8 << 20
        ),
        name="tiles_" + "_".join(str(back) for back in backs),
    )(index, starts, q, *ks, *vs, *state)


def first_starts(sizes, positions):
    order = jnp.arange(sizes.shape[0], dtype=jnp.int32)
    begins = jnp.sum(jnp.where(order[:, None] < order[None, :], sizes[:, None], 0), axis=0, dtype=jnp.int32)
    inside = begins[None, :] <= positions[:, None]
    return jnp.max(jnp.where(inside, begins[None, :], 0), axis=1)


def body(queries, keys, values, lengths):
    q, k, v = queries[0], keys[0], values[0]
    height = q.shape[0]
    index = lax.axis_index("seq").astype(jnp.int32)

    sizes = moved(lengths, step(0, 1))
    v_far = moved(v, back_two)
    k1 = moved(k, step(1, 1))
    v1 = moved(v, step(1, 1))
    q, k, v, sizes = lax.optimization_barrier((q, k, v, sizes))
    q0 = moved(q, step(0, 1))
    k0 = moved(k, step(0, 1))
    v0 = moved(v, step(0, 1))
    k2 = moved(k1, step(1))
    v2 = moved(v1, step(1))
    v4 = moved(v_far, back_four)
    k3 = moved(k2, step(1))
    v3 = moved(v4, step(-1))
    k4 = moved(k3, step(1))

    positions = index * height + jnp.arange(height, dtype=jnp.int32)
    starts = jnp.broadcast_to(first_starts(sizes[0], positions)[:, None], (height, HDIM))
    index = index.reshape(1)
    state = attention((0, 1, 2), index, starts, q0, [k0, k1, k2], [v0, v1, v2])
    return attention((3, 4), index, starts, q0, [k3, k4], [v3, v4], state, True)[None]


def solution(mesh):
    return jax.shard_map(
        body,
        mesh=mesh,
        in_specs=(
            P("section", "seq", None),
            P("section", "seq", None),
            P("section", "seq", None),
            P("section", None),
        ),
        out_specs=P("section", "seq", None),
        check_vma=False,
    )
```

```python
from functools import partial

import jax
import jax.numpy as jnp
from jax import lax
from jax.experimental import pallas as pl
from jax.experimental.pallas import tpu as pltpu
from jax.sharding import PartitionSpec as P

HDIM = 128
KV_HEADS = 4
GROUP = 5
RING = 8
LOWEST = -1e30
SCALE = HDIM**-0.5 * 1.4426950408889634


def moved(value, route):
    sections, blocks = lax.axis_size("section"), lax.axis_size("seq")
    pairs = []
    for s in range(sections):
        for b in range(blocks):
            s2, b2 = route(s, b)
            pairs.append((s * blocks + b, (s2 % sections) * blocks + b2 % blocks))
    return lax.ppermute(value, ("section", "seq"), pairs)


def step(blocks, sections=0):
    return lambda s, b: (s + sections, b + blocks)


def back_two(s, b):
    x, z = divmod(b + 4, RING)
    return s + 1, x * RING + (z + 2) % RING


def back_four(s, b):
    x, u = divmod(b, RING)
    return s, x * RING + (u - 2) % RING


def bias_of(starts, first_key, height):
    keys = first_key + lax.broadcasted_iota(jnp.int32, (height, height), 1)
    return jnp.where(keys >= starts, 0.0, LOWEST)


def tile(q, k, v, bias):
    height = bias.shape[0]
    raw = lax.dot_general(q, k, (((1,), (1,)), ((), ())), preferred_element_type=jnp.float32)
    raw = (raw.reshape(GROUP, height, height) + bias[None]).reshape(GROUP * height, height)
    top = jnp.max(raw, axis=1, keepdims=True)
    weights = jnp.exp2((raw - top) * SCALE)
    total = jnp.sum(weights, axis=1, keepdims=True)
    out = jnp.dot(weights.astype(jnp.bfloat16), v, preferred_element_type=jnp.float32)
    wide = (GROUP * height, HDIM)
    return out, jnp.broadcast_to(top, wide), jnp.broadcast_to(total, wide)


def merged(terms):
    highest = terms[0][1]
    for item in terms[1:]:
        highest = jnp.maximum(highest, item[1])
    out, total = None, None
    for tile_out, top, tile_sum in terms:
        factor = jnp.exp2((top - highest) * SCALE)
        part, part_sum = tile_out * factor, tile_sum * factor
        out = part if out is None else out + part
        total = part_sum if total is None else total + part_sum
    return out, highest, total


def kernel(backs, opening, closing, starts_ref, q_ref, *refs):
    count = len(backs)
    ks, vs, refs = refs[:count], refs[count : 2 * count], refs[2 * count :]
    state_in = () if opening else refs[:3]
    outs, bias_ref = refs[len(state_in) : -1], refs[-1]
    height = q_ref.shape[0]
    lane = lax.broadcasted_iota(jnp.int32, (height, HDIM), 1)
    digits = starts_ref[...].astype(jnp.float32) * jnp.where(lane == 0, 32.0, 1.0)
    distance = jnp.sum(digits, axis=1, keepdims=True).astype(jnp.int32)
    starts = lax.broadcasted_iota(jnp.int32, (height, 1), 0) - distance
    reach = jnp.sum(digits[:1]).astype(jnp.int32)

    def run(taken):
        for i in taken:
            back = backs[i]
            bias = bias_of(starts, -back * height, height)
            if back == 0:
                rows = lax.broadcasted_iota(jnp.int32, (height, height), 0)
                columns = lax.broadcasted_iota(jnp.int32, (height, height), 1)
                bias = jnp.where(columns <= rows, bias, LOWEST)
            bias_ref[i] = bias

        @pl.loop(0, KV_HEADS, unroll=KV_HEADS)
        def _(a):
            lanes = pl.ds(pl.multiple_of(a * HDIM, HDIM), HDIM)
            heads = [pl.ds(pl.multiple_of((a * GROUP + g) * HDIM, HDIM), HDIM) for g in range(GROUP)]
            terms = [tuple(ref[a] for ref in state_in)] if state_in else []
            if taken:
                q = jnp.concatenate([q_ref[:, h] for h in heads], axis=0)
                terms += [tile(q, ks[i][:, lanes], vs[i][:, lanes], bias_ref[i]) for i in taken]
            result = merged(terms)
            if closing:
                done = (result[0] / result[2]).astype(jnp.bfloat16)
                for g in range(GROUP):
                    outs[0][:, heads[g]] = done[g * height : (g + 1) * height]
            else:
                for ref, part in zip(outs, result):
                    ref[a] = part

    least = 1 if opening else 0
    for taken in range(least, count + 1):
        low = reach > (backs[taken - 1] - 1) * height if taken > least else True
        high = reach <= (backs[taken] - 1) * height if taken < count else True
        pl.when(jnp.logical_and(low, high))(partial(run, tuple(range(taken))))


def attention(backs, starts, q, ks, vs, state=(), closing=False):
    height = q.shape[0]
    count = len(backs)
    pairs = KV_HEADS * GROUP * height * height * count
    vmem = pl.BlockSpec(memory_space=pltpu.VMEM)
    part = jax.ShapeDtypeStruct((KV_HEADS, GROUP * height, HDIM), jnp.float32)
    first = 2 + 2 * count
    return pl.pallas_call(
        partial(kernel, backs, not state, closing),
        in_specs=[vmem] * (first + len(state)),
        out_specs=vmem if closing else [vmem] * 3,
        out_shape=jax.ShapeDtypeStruct(q.shape, jnp.bfloat16) if closing else [part] * 3,
        input_output_aliases={first + i: i for i in range(len(state))} if not closing else {},
        scratch_shapes=[pltpu.VMEM((count, height, height), jnp.float32)],
        compiler_params=pltpu.CompilerParams(vmem_limit_bytes=14 << 20),
        cost_estimate=pl.CostEstimate(
            flops=4 * HDIM * pairs, transcendentals=pairs, bytes_accessed=8 << 20
        ),
        name="tiles_" + "_".join(str(back) for back in backs),
    )(starts, q, *ks, *vs, *state)


def distances(sizes, positions):
    order = jnp.arange(sizes.shape[0], dtype=jnp.int32)
    begins = jnp.sum(jnp.where(order[:, None] < order[None, :], sizes[:, None], 0), axis=0, dtype=jnp.int32)
    inside = begins[None, :] <= positions[:, None]
    distance = positions - jnp.max(jnp.where(inside, begins[None, :], 0), axis=1)
    lane = jnp.arange(HDIM, dtype=jnp.int32)[None, :]
    digits = jnp.where(lane == 0, distance[:, None] // 32, jnp.where(lane == 1, distance[:, None] % 32, 0))
    return digits.astype(jnp.bfloat16)


def body(queries, keys, values, lengths):
    q, k, v = queries[0], keys[0], values[0]
    height = q.shape[0]
    index = lax.axis_index("seq").astype(jnp.int32)

    width = k.shape[1]
    positions = index * height + jnp.arange(height, dtype=jnp.int32)
    v_far = moved(v, back_two)
    k1 = moved(k, step(1, 1))
    v1 = moved(v, step(1, 1))
    q0 = moved(q, step(0, 1))
    near = moved(jnp.concatenate([k, v, distances(lengths[0], positions)], axis=1), step(0, 1))
    k0, v0, starts = near[:, :width], near[:, width : 2 * width], near[:, 2 * width :]
    k2 = moved(k1, step(1))
    v_far, v1 = lax.optimization_barrier((v_far, v1))
    v4 = moved(v_far, back_four)
    v2 = moved(v1, step(1))
    k3 = moved(k2, step(1))
    v3 = moved(v4, step(-1))
    k4 = moved(k3, step(1))
    state = attention((0, 1, 2), starts, q0, [k0, k1, k2], [v0, v1, v2])
    return attention((3, 4), starts, q0, [k3, k4], [v3, v4], state, True)[None]


def solution(mesh):
    return jax.shard_map(
        body,
        mesh=mesh,
        in_specs=(
            P("section", "seq", None),
            P("section", "seq", None),
            P("section", "seq", None),
            P("section", None),
        ),
        out_specs=P("section", "seq", None),
        check_vma=False,
    )
```

```python
from functools import partial

import jax
import jax.numpy as jnp
from jax import lax
from jax.experimental import pallas as pl
from jax.experimental.pallas import tpu as pltpu
from jax.sharding import PartitionSpec as P

HDIM = 128
KV_HEADS = 4
GROUP = 5
RING = 8
LOWEST = -1e30
SCALE = HDIM**-0.5 * 1.4426950408889634


def moved(value, route):
    sections, blocks = lax.axis_size("section"), lax.axis_size("seq")
    pairs = []
    for s in range(sections):
        for b in range(blocks):
            s2, b2 = route(s, b)
            pairs.append((s * blocks + b, (s2 % sections) * blocks + b2 % blocks))
    return lax.ppermute(value, ("section", "seq"), pairs)


def step(blocks, sections=0):
    return lambda s, b: (s + sections, b + blocks)


def back_two(s, b):
    x, z = divmod(b + 4, RING)
    return s + 1, x * RING + (z + 2) % RING


def back_four(s, b):
    x, u = divmod(b, RING)
    return s, x * RING + (u - 2) % RING


def bias_of(starts, first_key, height):
    keys = first_key + lax.broadcasted_iota(jnp.int32, (height, height), 1)
    return jnp.where(keys >= starts, 0.0, LOWEST)


def tile(q, k, v, bias):
    height = bias.shape[0]
    raw = lax.dot_general(q, k, (((1,), (1,)), ((), ())), preferred_element_type=jnp.float32)
    raw = (raw.reshape(GROUP, height, height) + bias[None]).reshape(GROUP * height, height)
    top = jnp.max(raw, axis=1, keepdims=True)
    weights = jnp.exp2((raw - top) * SCALE)
    total = jnp.sum(weights, axis=1, keepdims=True)
    out = jnp.dot(weights.astype(jnp.bfloat16), v, preferred_element_type=jnp.float32)
    wide = (GROUP * height, HDIM)
    return out, jnp.broadcast_to(top, wide), jnp.broadcast_to(total, wide)


def merged(terms):
    highest = terms[0][1]
    for item in terms[1:]:
        highest = jnp.maximum(highest, item[1])
    out, total = None, None
    for tile_out, top, tile_sum in terms:
        factor = jnp.exp2((top - highest) * SCALE)
        part, part_sum = tile_out * factor, tile_sum * factor
        out = part if out is None else out + part
        total = part_sum if total is None else total + part_sum
    return out, highest, total


def kernel(backs, opening, closing, starts_ref, q_ref, *refs):
    count = len(backs)
    ks, vs, refs = refs[:count], refs[count : 2 * count], refs[2 * count :]
    state_in = () if opening else refs[:3]
    outs, bias_ref = refs[len(state_in) : -1], refs[-1]
    height = q_ref.shape[0]
    lane = lax.broadcasted_iota(jnp.int32, (height, HDIM), 1)
    digits = starts_ref[...].astype(jnp.float32) * jnp.where(lane == 0, 32.0, 1.0)
    distance = jnp.sum(digits, axis=1, keepdims=True).astype(jnp.int32)
    starts = lax.broadcasted_iota(jnp.int32, (height, 1), 0) - distance
    reach = jnp.sum(digits[:1]).astype(jnp.int32)

    def run(taken):
        for i in taken:
            back = backs[i]
            bias = bias_of(starts, -back * height, height)
            if back == 0:
                rows = lax.broadcasted_iota(jnp.int32, (height, height), 0)
                columns = lax.broadcasted_iota(jnp.int32, (height, height), 1)
                bias = jnp.where(columns <= rows, bias, LOWEST)
            bias_ref[i] = bias

        @pl.loop(0, KV_HEADS, unroll=KV_HEADS)
        def _(a):
            lanes = pl.ds(pl.multiple_of(a * HDIM, HDIM), HDIM)
            heads = [pl.ds(pl.multiple_of((a * GROUP + g) * HDIM, HDIM), HDIM) for g in range(GROUP)]
            terms = [tuple(ref[a] for ref in state_in)] if state_in else []
            if taken:
                q = jnp.concatenate([q_ref[:, h] for h in heads], axis=0)
                terms += [tile(q, ks[i][:, lanes], vs[i][:, lanes], bias_ref[i]) for i in taken]
            result = merged(terms)
            if closing:
                done = (result[0] / result[2]).astype(jnp.bfloat16)
                for g in range(GROUP):
                    outs[0][:, heads[g]] = done[g * height : (g + 1) * height]
            else:
                for ref, part in zip(outs, result):
                    ref[a] = part

    least = 1 if opening else 0
    for taken in range(least, count + 1):
        low = reach > (backs[taken - 1] - 1) * height if taken > least else True
        high = reach <= (backs[taken] - 1) * height if taken < count else True
        pl.when(jnp.logical_and(low, high))(partial(run, tuple(range(taken))))


def attention(backs, starts, q, ks, vs, state=(), closing=False):
    height = q.shape[0]
    count = len(backs)
    pairs = KV_HEADS * GROUP * height * height * count
    vmem = pl.BlockSpec(memory_space=pltpu.VMEM)
    part = jax.ShapeDtypeStruct((KV_HEADS, GROUP * height, HDIM), jnp.float32)
    first = 2 + 2 * count
    return pl.pallas_call(
        partial(kernel, backs, not state, closing),
        in_specs=[vmem] * (first + len(state)),
        out_specs=vmem if closing else [vmem] * 3,
        out_shape=jax.ShapeDtypeStruct(q.shape, jnp.bfloat16) if closing else [part] * 3,
        input_output_aliases={first + i: i for i in range(len(state))} if not closing else {},
        scratch_shapes=[pltpu.VMEM((count, height, height), jnp.float32)],
        compiler_params=pltpu.CompilerParams(vmem_limit_bytes=14 << 20),
        cost_estimate=pl.CostEstimate(
            flops=4 * HDIM * pairs, transcendentals=pairs, bytes_accessed=8 << 20
        ),
        name="tiles_" + "_".join(str(back) for back in backs),
    )(starts, q, *ks, *vs, *state)


def distances(sizes, positions):
    order = jnp.arange(sizes.shape[0], dtype=jnp.int32)
    begins = jnp.sum(jnp.where(order[:, None] < order[None, :], sizes[:, None], 0), axis=0, dtype=jnp.int32)
    inside = begins[None, :] <= positions[:, None]
    distance = positions - jnp.max(jnp.where(inside, begins[None, :], 0), axis=1)
    lane = jnp.arange(HDIM, dtype=jnp.int32)[None, :]
    digits = jnp.where(lane == 0, distance[:, None] // 32, jnp.where(lane == 1, distance[:, None] % 32, 0))
    return digits.astype(jnp.bfloat16)


def body(queries, keys, values, lengths):
    q, k, v = queries[0], keys[0], values[0]
    height = q.shape[0]
    index = lax.axis_index("seq").astype(jnp.int32)

    width = k.shape[1]
    positions = index * height + jnp.arange(height, dtype=jnp.int32)
    v_far = moved(v, back_two)
    k1 = moved(k, step(1, 1))
    v1 = moved(v, step(1, 1))
    sizes = lengths[0]
    q0 = moved(q, step(0, 1))
    k, v, sizes, k1 = lax.optimization_barrier((k, v, sizes, k1))
    k0 = moved(k, step(0, 1))
    near = moved(jnp.concatenate([v, distances(sizes, positions)], axis=1), step(0, 1))
    v0, starts = near[:, :width], near[:, width:]
    k2 = moved(k1, step(1))
    v4 = moved(v_far, back_four)
    v2 = moved(v1, step(1))
    k2, v_far, v1 = lax.optimization_barrier((k2, v_far, v1))
    k3 = moved(k2, step(1))
    v3 = moved(v4, step(-1))
    k3, v2 = lax.optimization_barrier((k3, v2))
    k3, k0 = lax.optimization_barrier((k3, k0))
    k4 = moved(k3, step(1))
    state = attention((0, 1, 2), starts, q0, [k0, k1, k2], [v0, v1, v2])
    return attention((3, 4), starts, q0, [k3, k4], [v3, v4], state, True)[None]


def solution(mesh):
    return jax.shard_map(
        body,
        mesh=mesh,
        in_specs=(
            P("section", "seq", None),
            P("section", "seq", None),
            P("section", "seq", None),
            P("section", None),
        ),
        out_specs=P("section", "seq", None),
        check_vma=False,
    )
```

```python
from functools import partial

import jax
import jax.numpy as jnp
from jax import lax
from jax.experimental import pallas as pl
from jax.experimental.pallas import tpu as pltpu
from jax.sharding import PartitionSpec as P

HDIM = 128
KV_HEADS = 4
GROUP = 5
RING = 8
LOWEST = -1e30
SCALE = HDIM**-0.5 * 1.4426950408889634


def moved(value, route):
    sections, blocks = lax.axis_size("section"), lax.axis_size("seq")
    pairs = []
    for s in range(sections):
        for b in range(blocks):
            s2, b2 = route(s, b)
            pairs.append((s * blocks + b, (s2 % sections) * blocks + b2 % blocks))
    return lax.ppermute(value, ("section", "seq"), pairs)


def step(blocks, sections=0):
    return lambda s, b: (s + sections, b + blocks)


def back_two(s, b):
    x, z = divmod(b + 4, RING)
    return s + 1, x * RING + (z + 2) % RING


def back_four(s, b):
    x, u = divmod(b, RING)
    return s, x * RING + (u - 2) % RING


def bias_of(starts, first_key, height):
    keys = first_key + lax.broadcasted_iota(jnp.int32, (height, height), 1)
    return jnp.where(keys >= starts, 0.0, LOWEST)


def tile(q, k, v, bias):
    rows, keys = bias.shape
    raw = lax.dot_general(q, k, (((1,), (1,)), ((), ())), preferred_element_type=jnp.float32)
    raw = (raw.reshape(GROUP, rows, keys) + bias[None]).reshape(GROUP * rows, keys)
    top = jnp.max(raw, axis=1, keepdims=True)
    weights = jnp.exp2((raw - top) * SCALE)
    total = jnp.sum(weights, axis=1, keepdims=True)
    out = jnp.dot(weights.astype(jnp.bfloat16), v, preferred_element_type=jnp.float32)
    wide = (GROUP * rows, HDIM)
    return out, jnp.broadcast_to(top, wide), jnp.broadcast_to(total, wide)


def merged(terms):
    highest = terms[0][1]
    for item in terms[1:]:
        highest = jnp.maximum(highest, item[1])
    out, total = None, None
    for tile_out, top, tile_sum in terms:
        factor = jnp.exp2((top - highest) * SCALE)
        part, part_sum = tile_out * factor, tile_sum * factor
        out = part if out is None else out + part
        total = part_sum if total is None else total + part_sum
    return out, highest, total


def kernel(backs, opening, closing, starts_ref, q_ref, *refs):
    count = len(backs)
    ks, vs, refs = refs[:count], refs[count : 2 * count], refs[2 * count :]
    state_in = () if opening else refs[:3]
    outs, bias_ref = refs[len(state_in) : -1], refs[-1]
    height = q_ref.shape[0]
    lane = lax.broadcasted_iota(jnp.int32, (height, HDIM), 1)
    digits = starts_ref[...].astype(jnp.float32) * jnp.where(lane == 0, 32.0, 1.0)
    distance = jnp.sum(digits, axis=1, keepdims=True).astype(jnp.int32)
    starts = lax.broadcasted_iota(jnp.int32, (height, 1), 0) - distance

    def run(taken, row, rows):
        for i in taken:
            back = backs[i]
            bias = bias_of(starts, -back * height, height)
            if back == 0:
                own = lax.broadcasted_iota(jnp.int32, (height, height), 0)
                columns = lax.broadcasted_iota(jnp.int32, (height, height), 1)
                bias = jnp.where(columns <= own, bias, LOWEST)
            bias_ref[i] = bias

        @pl.loop(0, KV_HEADS, unroll=KV_HEADS)
        def _(a):
            lanes = pl.ds(pl.multiple_of(a * HDIM, HDIM), HDIM)
            heads = [pl.ds(pl.multiple_of((a * GROUP + g) * HDIM, HDIM), HDIM) for g in range(GROUP)]
            part = [pl.ds(g * height + row, rows) for g in range(GROUP)]
            terms = []
            if state_in:
                terms.append([jnp.concatenate([ref[a, p] for p in part], axis=0) for ref in state_in])
            if taken:
                q = jnp.concatenate([q_ref[row : row + rows, h] for h in heads], axis=0)
                for i in taken:
                    terms.append(tile(q, ks[i][:, lanes], vs[i][:, lanes], bias_ref[i, row : row + rows]))
            result = merged(terms)
            if closing:
                done = (result[0] / result[2]).astype(jnp.bfloat16)
                for g in range(GROUP):
                    outs[0][row : row + rows, heads[g]] = done[g * rows : (g + 1) * rows]
            else:
                for ref, value in zip(outs, result):
                    for g in range(GROUP):
                        ref[a, part[g]] = value[g * rows : (g + 1) * rows]

    least = 1 if opening else 0
    rows = height // 2 if closing else height
    for row in range(0, height, rows):
        reach = jnp.sum(digits[row : row + 1]).astype(jnp.int32) - row
        for taken in range(least, count + 1):
            low = reach > (backs[taken - 1] - 1) * height if taken > least else True
            high = reach <= (backs[taken] - 1) * height if taken < count else True
            pl.when(jnp.logical_and(low, high))(partial(run, tuple(range(taken)), row, rows))


def attention(backs, starts, q, ks, vs, state=(), closing=False):
    height = q.shape[0]
    count = len(backs)
    pairs = KV_HEADS * GROUP * height * height * count
    vmem = pl.BlockSpec(memory_space=pltpu.VMEM)
    part = jax.ShapeDtypeStruct((KV_HEADS, GROUP * height, HDIM), jnp.float32)
    first = 2 + 2 * count
    return pl.pallas_call(
        partial(kernel, backs, not state, closing),
        in_specs=[vmem] * (first + len(state)),
        out_specs=vmem if closing else [vmem] * 3,
        out_shape=jax.ShapeDtypeStruct(q.shape, jnp.bfloat16) if closing else [part] * 3,
        input_output_aliases={first + i: i for i in range(len(state))} if not closing else {},
        scratch_shapes=[pltpu.VMEM((count, height, height), jnp.float32)],
        compiler_params=pltpu.CompilerParams(vmem_limit_bytes=14 << 20),
        cost_estimate=pl.CostEstimate(
            flops=4 * HDIM * pairs, transcendentals=pairs, bytes_accessed=8 << 20
        ),
        name="tiles_" + "_".join(str(back) for back in backs),
    )(starts, q, *ks, *vs, *state)


def distances(sizes, positions):
    order = jnp.arange(sizes.shape[0], dtype=jnp.int32)
    begins = jnp.sum(jnp.where(order[:, None] < order[None, :], sizes[:, None], 0), axis=0, dtype=jnp.int32)
    inside = begins[None, :] <= positions[:, None]
    distance = positions - jnp.max(jnp.where(inside, begins[None, :], 0), axis=1)
    lane = jnp.arange(HDIM, dtype=jnp.int32)[None, :]
    digits = jnp.where(lane == 0, distance[:, None] // 32, jnp.where(lane == 1, distance[:, None] % 32, 0))
    return digits.astype(jnp.bfloat16)


def body(queries, keys, values, lengths):
    q, k, v = queries[0], keys[0], values[0]
    height = q.shape[0]
    index = lax.axis_index("seq").astype(jnp.int32)

    width = k.shape[1]
    positions = index * height + jnp.arange(height, dtype=jnp.int32)
    v_far = moved(v, back_two)
    k1 = moved(k, step(1, 1))
    v1 = moved(v, step(1, 1))
    sizes = lengths[0]
    q0 = moved(q, step(0, 1))
    k, v, sizes, k1 = lax.optimization_barrier((k, v, sizes, k1))
    k0 = moved(k, step(0, 1))
    near = moved(jnp.concatenate([v, distances(sizes, positions)], axis=1), step(0, 1))
    v0, starts = near[:, :width], near[:, width:]
    k2 = moved(k1, step(1))
    v4 = moved(v_far, back_four)
    v2 = moved(v1, step(1))
    k2, v_far, v1 = lax.optimization_barrier((k2, v_far, v1))
    k3 = moved(k2, step(1))
    v3 = moved(v4, step(-1))
    k3, v2 = lax.optimization_barrier((k3, v2))
    k3, k0 = lax.optimization_barrier((k3, k0))
    k4 = moved(k3, step(1))
    state = attention((0, 1, 2), starts, q0, [k0, k1, k2], [v0, v1, v2])
    return attention((3, 4), starts, q0, [k3, k4], [v3, v4], state, True)[None]


def solution(mesh):
    return jax.shard_map(
        body,
        mesh=mesh,
        in_specs=(
            P("section", "seq", None),
            P("section", "seq", None),
            P("section", "seq", None),
            P("section", None),
        ),
        out_specs=P("section", "seq", None),
        check_vma=False,
    )
```
